512 devices in a mesh: section: 32 (over z, core), tensor: 8 (over x, y_lo), replica: 2 (over y_hi).
Axes of the slice: x: 4, y: 4 (y_hi: 2, y_lo: 2; y = y_hi * 2 + y_lo), z: 16, core: 2. Of those that a mesh axis runs over, the one named last changes fastest.
Arguments:
- pool_inputs: bfloat16 [32, 256, 2, 1408], P('section', 'replica', None, 'tensor'), may hold values from -6 to 6
- pool_mixed: bfloat16 [32, 256, 1408], P('section', 'replica'), may hold values from -6 to 6
- crop_ids: int32 [32, 8, 128], P('section', 'replica'), may hold values from 0 to 127
- incoming: bfloat16 [32, 256, 1408], P('section', 'replica', 'tensor'), may hold values from -6 to 6
- loss_grads: bfloat16 [3, 256, 1408], P(None, 'replica', 'tensor'), may hold values from -6 to 6
- w_proj: bfloat16 [32, 2, 1408, 1408], P('section', None, ('tensor', 'replica')), may hold values from -0.109375 to 0.109375
- w_up: bfloat16 [32, 1408, 3072], P('section', None, ('tensor', 'replica')), may hold values from -0.15625 to 0.15625
- w_down: bfloat16 [32, 3072, 1408], P('section', ('tensor', 'replica')), may hold values from -0.109375 to 0.109375
Outputs:
- grad_proj: bfloat16 [32, 2, 1408, 1408], P('section', None, ('tensor', 'replica'))
- grad_up: bfloat16 [32, 1408, 3072], P('section', None, ('tensor', 'replica'))
- grad_down: bfloat16 [32, 3072, 1408], P('section', ('tensor', 'replica'))
- outgoing: bfloat16 [32, 256, 2, 1408], P('section', 'replica', None, 'tensor')
The draws below stay inside these ranges and needn't reach their ends.
All inputs are finite; a program needn't handle non-finite values.
Results may differ from the reference program's by a relative error of at most 0.02.
Values may be sent and summed in bfloat16 or wider, within the bound.
No kernel may reach another device: no remote copies, remote signals or barrier semaphores. Data moves between devices by JAX's collectives and lax.ppermute only.
A program may use at most 64 MiB of HBM per device.

```python
import math
import jax
import jax.numpy as jnp
import numpy as np
from jax import lax

D = 1408
FF = 3072
M = 128
TICKS = 4
POOL = 128
SECTIONS = 32
REPLICAS = 2


def set_ends(drawn, stream_key, low, high):
    longest = drawn.shape.index(max(drawn.shape))
    spots = []
    for shift in (0, 1):
        where = [jax.random.randint(jax.random.fold_in(stream_key, axis), (), 0, length) for axis, length in enumerate(drawn.shape)]
        where[longest] = (where[longest] + shift) % drawn.shape[longest]
        spots.append(tuple(where))
    return drawn.at[spots[0]].set(low).at[spots[1]].set(high)


def shard_levels(stream_key, dims, cuts, smallest, top_value):
    factor_of, own = 1.0, jax.random.fold_in(stream_key, 6)
    for position, shards_of in cuts:
        draws = jnp.exp(jax.random.uniform(jax.random.fold_in(own, position), (shards_of,), jnp.float32, smallest / len(cuts), top_value / len(cuts)))
        factor_of = factor_of * jnp.repeat(draws, dims[position] // shards_of).reshape([-1 if axis == position else 1 for axis in range(len(dims))])
    return factor_of


def rank_bounds(count, lean):
    loads = [(1 << 20) // math.isqrt(rank ** lean) + 1 for rank in range(1, count + 1)]
    width = 1 + sum(loads) // (1 << 30)
    return np.cumsum(np.array([max(1, weight // width) for weight in loads]))


def ranked(key, shape, number_of, slope):
    listing = rank_bounds(number_of, slope)
    lot = jax.random.randint(jax.random.fold_in(key, 1), shape, 0, int(listing[number_of - 1]))
    rank = jnp.searchsorted(jnp.asarray(listing, jnp.int32), lot, side="right")
    return jax.random.permutation(jax.random.fold_in(key, 2), number_of)[rank].astype(jnp.int32)


def noise(rng, extent, width, limit, split=(), kind=jnp.bfloat16):
    factor_of = shard_levels(rng, extent, split, -0.22, 0.18) if split else 1.0
    array = jax.random.normal(rng, extent, jnp.float32) * width * factor_of
    return jnp.minimum(jnp.maximum(array, -limit), limit).astype(kind)


def setup_inputs(seed: int = 0) -> dict:
    key_of = jax.random.split(jax.random.key(seed), 9)
    return {
        "pool_inputs": noise(key_of[0], (SECTIONS, REPLICAS * POOL, 2, D), 1.0, 6.0, ((0, 32), (1, 2), (3, 8))),
        "pool_mixed": noise(key_of[1], (SECTIONS, REPLICAS * POOL, D), 1.0, 6.0, ((0, 32), (1, 2))),
        "crop_ids": set_ends(ranked(key_of[2], (SECTIONS, REPLICAS * TICKS, M), POOL, 2), jax.random.fold_in(key_of[2], 3), 0, POOL - 1).astype(jnp.int32),
        "incoming": noise(key_of[3], (SECTIONS, REPLICAS * M, D), 1.0, 6.0, ((0, 32), (1, 2), (2, 8))),
        "loss_grads": noise(key_of[4], (TICKS - 1, REPLICAS * M, D), 1.0, 6.0, ((1, 2), (2, 8))),
        "w_proj": noise(key_of[5], (SECTIONS, 2, D, D), (2 * D) ** -0.5, 0.109375, ((0, 32), (2, 16))),
        "w_up": noise(key_of[6], (SECTIONS, D, FF), D ** -0.5, 0.15625, ((0, 32), (2, 16))),
        "w_down": noise(key_of[7], (SECTIONS, FF, D), FF ** -0.5, 0.109375, ((0, 32), (1, 16))),
    }


gelu_scale = 0.7978845608
gelu_cubic = 0.044715


def gelu_pair(pre_gelu):
    inner = gelu_scale * (pre_gelu + gelu_cubic * pre_gelu * pre_gelu * pre_gelu)
    tanh_part = jnp.tanh(inner)
    gelu_value = 0.5 * pre_gelu * (1.0 + tanh_part)
    gelu_slope = 0.5 * (1.0 + tanh_part) + 0.5 * pre_gelu * (1.0 - tanh_part * tanh_part) * gelu_scale * (1.0 + 3.0 * gelu_cubic * pre_gelu * pre_gelu)
    return gelu_value, gelu_slope


def section_back(proj_weight, up_weight, down_weight, inputs, mixed_rows, upstream):
    pre_gelu = jnp.dot(mixed_rows, up_weight, preferred_element_type=jnp.float32)
    gelu_value, gelu_slope = gelu_pair(pre_gelu)
    activated = gelu_value.astype(jnp.bfloat16)
    back_act = jnp.dot(upstream, down_weight.T, preferred_element_type=jnp.float32)
    back_hidden = (back_act * gelu_slope).astype(jnp.bfloat16)
    back_mixed = upstream.astype(jnp.float32) + jnp.dot(back_hidden, up_weight.T, preferred_element_type=jnp.float32)
    mixed_grad = back_mixed.astype(jnp.bfloat16)
    input_grad = jnp.einsum('mj,kij->mki', mixed_grad.astype(jnp.float32), proj_weight.astype(jnp.float32)).astype(jnp.bfloat16)
    return activated, back_hidden, mixed_grad, input_grad


def finish(total):
    rounded = lax.optimization_barrier(total.astype(jnp.bfloat16))
    return jnp.sum(rounded.astype(jnp.float32), axis=0).astype(jnp.bfloat16)


def reference(pool_inputs, pool_mixed, crop_ids, incoming, loss_grads, w_proj, w_up, w_down):
    section_ids = jnp.arange(SECTIONS, dtype=jnp.int32)
    decoder_flag = (section_ids >= SECTIONS // 2).astype(jnp.float32)
    skip_mask = jnp.stack([jnp.ones((SECTIONS,), jnp.float32), decoder_flag], axis=1).astype(jnp.bfloat16)[:, None, :, None]
    encoder_weight = (section_ids < SECTIONS // 2).astype(jnp.float32)[:, None, None]
    offsets = (jnp.arange(REPLICAS, dtype=jnp.int32) * POOL)[None, :, None, None]
    row_ids = crop_ids.reshape(SECTIONS, REPLICAS, TICKS, M).astype(jnp.int32) + offsets
    upstream = incoming
    seen_inputs, seen_mixed, seen_upstream = [], [], []
    input_grad = None
    for tick_index in range(TICKS):
        picked_rows = row_ids[:, :, tick_index, :].reshape(SECTIONS, REPLICAS * M)
        inputs = jax.vmap(lambda source_rows, chosen: source_rows[chosen])(pool_inputs, picked_rows) * skip_mask
        mixed_rows = jax.vmap(lambda source_rows, chosen: source_rows[chosen])(pool_mixed, picked_rows)
        seen_inputs.append(inputs)
        seen_mixed.append(mixed_rows)
        seen_upstream.append(upstream)
        input_grad = lax.map(lambda packed: section_back(*packed)[3], (w_proj, w_up, w_down, inputs, mixed_rows, upstream))
        if tick_index + 1 < TICKS:
            below_grad = input_grad[:, :, 0]
            skip_grad = input_grad[:, :, 1]
            from_above = jnp.concatenate([below_grad[1:], jnp.zeros_like(below_grad[:1])], axis=0)
            mirrored = skip_grad[::-1]
            upstream = (from_above.astype(jnp.float32) + encoder_weight * mirrored.astype(jnp.float32)).astype(jnp.bfloat16)
            upstream = upstream.at[SECTIONS - 1].set(loss_grads[tick_index])
    all_inputs = jnp.stack(seen_inputs, axis=1)
    all_mixed = jnp.stack(seen_mixed, axis=1)
    all_upstream = jnp.stack(seen_upstream, axis=1)

    def section_grads(packed):
        proj_weight, up_weight, down_weight, inputs_ticks, mixed_ticks, upstream_ticks = packed
        proj_total = jnp.zeros((REPLICAS, 2, D, D), jnp.float32)
        up_total = jnp.zeros((REPLICAS, D, FF), jnp.float32)
        down_total = jnp.zeros((REPLICAS, FF, D), jnp.float32)
        for tick_index in range(TICKS):
            inputs = inputs_ticks[tick_index]
            mixed_rows = mixed_ticks[tick_index]
            upstream_now = upstream_ticks[tick_index]
            activated, back_hidden, mixed_grad, unused_grad = section_back(proj_weight, up_weight, down_weight, inputs, mixed_rows, upstream_now)
            down_total = down_total + jnp.einsum('rmf,rmd->rfd', activated.reshape(REPLICAS, M, FF).astype(jnp.float32), upstream_now.reshape(REPLICAS, M, D).astype(jnp.float32))
            up_total = up_total + jnp.einsum('rmd,rmf->rdf', mixed_rows.reshape(REPLICAS, M, D).astype(jnp.float32), back_hidden.reshape(REPLICAS, M, FF).astype(jnp.float32))
            proj_total = proj_total + jnp.einsum('rmki,rmj->rkij', inputs.reshape(REPLICAS, M, 2, D).astype(jnp.float32), mixed_grad.reshape(REPLICAS, M, D).astype(jnp.float32))
        return finish(proj_total), finish(up_total), finish(down_total)

    grad_proj, grad_up, grad_down = lax.map(section_grads, (w_proj, w_up, w_down, all_inputs, all_mixed, all_upstream))
    return grad_proj, grad_up, grad_down, input_grad
```

```python
import jax
import jax.numpy as jnp
from jax import lax
from jax.sharding import PartitionSpec as P

gelu_scale = 0.7978845608
gelu_cubic = 0.044715
f32 = jnp.float32
bf16 = jnp.bfloat16


def gelu_pair(pre_gelu):
    inner = gelu_scale * (pre_gelu + gelu_cubic * pre_gelu * pre_gelu * pre_gelu)
    tanh_part = jnp.tanh(inner)
    gelu_value = 0.5 * pre_gelu * (1.0 + tanh_part)
    gelu_slope = 0.5 * (1.0 + tanh_part) + 0.5 * pre_gelu * (
        1.0 - tanh_part * tanh_part
    ) * gelu_scale * (1.0 + 3.0 * gelu_cubic * pre_gelu * pre_gelu)
    return (gelu_value, gelu_slope)


def dot(a, b, ca=1, cb=0):
    return lax.dot_general(a, b, (((ca,), (cb,)), ((), ())), preferred_element_type=f32)


def swap(x):
    return lax.ppermute(x, "replica", [(0, 1), (1, 0)])


def gather(chunk, axes="tensor"):
    count = lax.axis_size(axes)
    spread = jnp.broadcast_to(chunk[None], (count, *chunk.shape))
    return lax.all_to_all(spread, axes, 0, 0)


def body(pool_inputs, pool_mixed, crop_ids, incoming, loss_grads, w_proj, w_up, w_down):
    section = lax.axis_index("section")
    sections = lax.axis_size("section")
    replica = lax.axis_index("replica")
    parts = lax.axis_size("tensor")
    half = sections // 2
    first = replica == 0
    is_top = section == sections - 1
    ticks, rows = crop_ids.shape[1:]
    pool = pool_mixed.shape[1]
    width = pool_mixed.shape[2]
    units = w_down.shape[1]
    own_in = w_proj.shape[2]
    chunk_rows = incoming.shape[2]

    def by_replica(own, other):
        return jnp.where(first, own, other), jnp.where(first, other, own)

    up_other = swap(w_up[0])
    down_other = swap(w_down[0])
    proj_other = swap(w_proj[0])
    mixed_other = swap(pool_mixed[0])
    ids_other = swap(crop_ids[0, ticks - 1])

    chunk = incoming[0].T
    upstream = gather(chunk).reshape(width, rows)

    up = jnp.concatenate([w_up[0], up_other], axis=1)
    down = jnp.concatenate([w_down[0], down_other], axis=0)
    proj = jnp.concatenate(by_replica(w_proj[0], proj_other), axis=1).reshape(-1, width)

    places = jnp.arange(pool, dtype=jnp.int32)[:, None]
    pick = (crop_ids[0].reshape(1, -1) == places).astype(bf16)
    pick_other = (ids_other[None, :] == places).astype(bf16)

    def picked(t):
        return pick[:, t * rows : (t + 1) * rows]

    pre = dot(up, pool_mixed[0], 0, 1)
    value, slope = gelu_pair(pre)
    active = value.astype(bf16)
    high = slope.astype(bf16)
    low = (slope - high.astype(f32)).astype(bf16)
    slopes = dot(high, pick) + dot(low, pick)

    decoder = jnp.where(section < half, 0.0, 1.0).astype(bf16)
    mask = jnp.stack([jnp.ones((), bf16), decoder])[:, None, None]
    saved = pool_inputs[0].transpose(1, 2, 0) * mask
    saved_first, saved_second = saved[:, :own_in], saved[:, own_in:]
    saved_own = jnp.where(first, saved_first, saved_second).reshape(-1, pool)
    saved_sent = jnp.where(first, saved_second, saved_first).reshape(-1, pool)
    saved_other = swap(saved_sent)
    last_own = dot(saved_own, picked(ticks - 1)).astype(bf16)
    last_other = dot(saved_other, pick_other).astype(bf16)
    active_other = swap(active[units:])

    hiddens, grads, upstreams = [], [], []
    for t in range(ticks):
        upstreams.append(upstream)
        if t + 1 == ticks:
            seen = dot(jnp.concatenate(upstreams, axis=1), pick, 1, 1).astype(bf16)
            seen_other = swap(seen)
            early = dot(
                jnp.concatenate(grads, axis=1), pick[:, : t * rows], 1, 1
            ).astype(bf16)
            early_other = swap(early)
        slope_now = slopes[:, t * rows : (t + 1) * rows]
        hidden = (dot(down, upstream) * slope_now).astype(bf16)
        hiddens.append(hidden)
        partial = dot(up, hidden).astype(bf16)
        terms = lax.all_to_all(partial.reshape(parts, chunk_rows, rows), "tensor", 0, 0)
        mixed_chunk = (
            jnp.sum(terms.astype(f32), axis=0) + chunk.astype(f32)
        ).astype(bf16)
        if t + 1 < ticks:
            mixed_grad = gather(mixed_chunk).reshape(width, rows)
            grads.append(mixed_grad)
            input_grad = dot(proj, mixed_grad).astype(bf16).reshape(2, chunk_rows, rows)
            above = lax.ppermute(
                input_grad[0], "section", [(i, i - 1) for i in range(1, sections)]
            )
            mirrored = lax.ppermute(
                input_grad[1],
                "section",
                [(i, sections - 1 - i) for i in range(half, sections)],
            )
            summed = (above.astype(f32) + mirrored.astype(f32)).astype(bf16)
            chunk = jnp.where(is_top, loss_grads[t].T, summed)
            upstream = gather(chunk).reshape(width, rows)
        else:
            spread = dot(jnp.concatenate(hiddens, axis=1), pick, 1, 1).astype(bf16)
            spread_other = swap(spread[units:])
            both = gather(mixed_chunk, ("replica", "tensor")).reshape(2, width, rows)
            mixed_grad = jnp.where(first, both[0], both[1])
            input_grad = dot(proj, mixed_grad).astype(bf16).reshape(2, chunk_rows, rows)

    grad_up = dot(
        jnp.concatenate([pool_mixed[0], mixed_other], axis=0),
        jnp.concatenate([spread[:units], spread_other], axis=1),
        0,
        1,
    ).astype(bf16)
    grad_down = dot(
        jnp.concatenate([active[:units], active_other], axis=1),
        jnp.concatenate([seen, seen_other], axis=1),
        1,
        1,
    ).astype(bf16)
    grad_proj = dot(
        jnp.concatenate(
            [saved_own, saved_other, *by_replica(last_own, last_other)], axis=1
        ),
        jnp.concatenate([early, early_other, both[0], both[1]], axis=1),
        1,
        1,
    ).astype(bf16)
    return (
        grad_proj.reshape(1, 2, own_in, width),
        grad_up[None],
        grad_down[None],
        input_grad.transpose(2, 0, 1)[None],
    )


def solution(mesh):
    in_specs = (
        P("section", "replica", None, "tensor"),
        P("section", "replica", None),
        P("section", "replica", None),
        P("section", "replica", "tensor"),
        P(None, "replica", "tensor"),
        P("section", None, ("tensor", "replica"), None),
        P("section", None, ("tensor", "replica")),
        P("section", ("tensor", "replica"), None),
    )
    out_specs = (
        P("section", None, ("tensor", "replica"), None),
        P("section", None, ("tensor", "replica")),
        P("section", ("tensor", "replica"), None),
        P("section", "replica", None, "tensor"),
    )
    return jax.shard_map(body, mesh=mesh, in_specs=in_specs, out_specs=out_specs, check_vma=False)
```

```python
import jax
import jax.numpy as jnp
from jax import lax
from jax.sharding import PartitionSpec as P

gelu_scale = 0.7978845608
gelu_cubic = 0.044715
f32 = jnp.float32
bf16 = jnp.bfloat16


def gelu_pair(pre_gelu):
    inner = gelu_scale * (pre_gelu + gelu_cubic * pre_gelu * pre_gelu * pre_gelu)
    tanh_part = jnp.tanh(inner)
    gelu_value = 0.5 * pre_gelu * (1.0 + tanh_part)
    gelu_slope = 0.5 * (1.0 + tanh_part) + 0.5 * pre_gelu * (
        1.0 - tanh_part * tanh_part
    ) * gelu_scale * (1.0 + 3.0 * gelu_cubic * pre_gelu * pre_gelu)
    return (gelu_value, gelu_slope)


def dot(a, b, ca=1, cb=0):
    return lax.dot_general(a, b, (((ca,), (cb,)), ((), ())), preferred_element_type=f32)


def swap(x):
    return lax.ppermute(x, "replica", [(0, 1), (1, 0)])


def gather(chunk, axes="tensor"):
    count = lax.axis_size(axes)
    spread = jnp.broadcast_to(chunk[None], (count, *chunk.shape))
    return lax.all_to_all(spread, axes, 0, 0)


def body(pool_inputs, pool_mixed, crop_ids, incoming, loss_grads, w_proj, w_up, w_down):
    section = lax.axis_index("section")
    sections = lax.axis_size("section")
    replica = lax.axis_index("replica")
    parts = lax.axis_size("tensor")
    half = sections // 2
    first = replica == 0
    is_top = section == sections - 1
    ticks, rows = crop_ids.shape[1:]
    pool = pool_mixed.shape[1]
    width = pool_mixed.shape[2]
    units = w_down.shape[1]
    own_in = w_proj.shape[2]
    chunk_rows = incoming.shape[2]

    def by_replica(own, other):
        return jnp.where(first, own, other), jnp.where(first, other, own)

    def tied(*values):
        return lax.optimization_barrier(values)

    up_other = swap(w_up[0])
    down_other = swap(w_down[0])
    chunk = incoming[0].T
    upstream = gather(chunk).reshape(width, rows)
    upstream, proj_own = tied(upstream, w_proj[0])
    proj_other = swap(proj_own)

    up = jnp.concatenate([w_up[0], up_other], axis=1)
    down = jnp.concatenate([w_down[0], down_other], axis=0)
    proj = jnp.concatenate(by_replica(proj_own, proj_other), axis=1).reshape(-1, width)

    places = jnp.arange(pool, dtype=jnp.int32)[:, None]
    pick = [(ids[None, :] == places).astype(bf16) for ids in crop_ids[0]]

    pre = dot(up, pool_mixed[0], 0, 1)
    value, slope = gelu_pair(pre)
    active = value.astype(bf16)
    high = slope.astype(bf16)
    low = (slope - high.astype(f32)).astype(bf16)

    decoder = jnp.where(section < half, 0.0, 1.0).astype(bf16)
    mask = jnp.stack([jnp.ones((), bf16), decoder])[:, None, None]
    saved = pool_inputs[0].transpose(1, 2, 0) * mask
    saved_first, saved_second = saved[:, :own_in], saved[:, own_in:]
    saved_own = jnp.where(first, saved_first, saved_second).reshape(-1, pool)
    saved_sent = jnp.where(first, saved_second, saved_first).reshape(-1, pool)
    ids_sent = jnp.broadcast_to(crop_ids[0, ticks - 1].astype(bf16)[None], (16, rows))
    small = jnp.concatenate([saved_sent, active[units:], ids_sent], axis=0)

    seen, spread, early = 0.0, 0.0, 0.0
    for t in range(ticks):
        slope_now = dot(high, pick[t]) + dot(low, pick[t])
        hidden = (dot(down, upstream) * slope_now).astype(bf16)
        partial = dot(up, hidden).astype(bf16)
        terms = lax.all_to_all(partial.reshape(parts, chunk_rows, rows), "tensor", 0, 0)
        upstream_late, hidden_late, _ = tied(upstream, hidden, partial)
        seen = seen + dot(upstream_late, pick[t], 1, 1)
        spread = spread + dot(hidden_late, pick[t], 1, 1)
        if t + 1 == ticks:
            seen = seen.astype(bf16)
            seen_other = swap(seen)
            spread = spread.astype(bf16)
            spread_other = swap(spread[units:])
            terms, seen_other, spread_other = tied(terms, seen_other, spread_other)
        mixed_chunk = (
            jnp.sum(terms.astype(f32), axis=0) + chunk.astype(f32)
        ).astype(bf16)
        if t + 1 < ticks:
            mixed_grad = gather(mixed_chunk).reshape(width, rows)
            early = early + dot(mixed_grad, pick[t], 1, 1)
            input_grad = dot(proj, mixed_grad).astype(bf16).reshape(2, chunk_rows, rows)
            above = lax.ppermute(
                input_grad[0], "section", [(i, i - 1) for i in range(1, sections)]
            )
            mirrored = lax.ppermute(
                input_grad[1],
                "section",
                [(i, sections - 1 - i) for i in range(half, sections)],
            )
            if t == 0:
                mixed_own, _ = tied(pool_mixed[0], mixed_grad)
                sent = swap(mixed_own)
            elif t == 1:
                small, _ = tied(small, mixed_grad)
                sent = swap(small)
            else:
                early = early.astype(bf16)
                sent = swap(early)
            summed = (above.astype(f32) + mirrored.astype(f32)).astype(bf16)
            chunk = jnp.where(is_top, loss_grads[t].T, summed)
            upstream = gather(chunk).reshape(width, rows)
            upstream, sent = tied(upstream, sent)
            if t == 0:
                mixed_other = sent
            elif t == 1:
                count = saved_own.shape[0]
                saved_other = sent[:count]
                active_other = sent[count : count + units]
                ids_other = sent[count + units].astype(jnp.int32)
                pick_other = (ids_other[None, :] == places).astype(bf16)
                last_own = dot(saved_own, pick[ticks - 1]).astype(bf16)
                last_other = dot(saved_other, pick_other).astype(bf16)
            else:
                early_other = sent
        else:
            both = gather(mixed_chunk, ("replica", "tensor")).reshape(2, width, rows)
            input_grad = jnp.where(first, dot(proj, both[0]), dot(proj, both[1]))
            input_grad = input_grad.astype(bf16).reshape(2, chunk_rows, rows)

    grad_up = dot(
        jnp.concatenate([pool_mixed[0], mixed_other], axis=0),
        jnp.concatenate([spread[:units], spread_other], axis=1),
        0,
        1,
    ).astype(bf16)
    grad_down = dot(
        jnp.concatenate([active[:units], active_other], axis=1),
        jnp.concatenate([seen, seen_other], axis=1),
        1,
        1,
    ).astype(bf16)
    grad_proj = dot(
        jnp.concatenate(
            [saved_own, saved_other, *by_replica(last_own, last_other)], axis=1
        ),
        jnp.concatenate([early, early_other, both[0], both[1]], axis=1),
        1,
        1,
    ).astype(bf16)
    return (
        grad_proj.reshape(1, 2, own_in, width),
        grad_up[None],
        grad_down[None],
        input_grad.transpose(2, 0, 1)[None],
    )


def solution(mesh):
    in_specs = (
        P("section", "replica", None, "tensor"),
        P("section", "replica", None),
        P("section", "replica", None),
        P("section", "replica", "tensor"),
        P(None, "replica", "tensor"),
        P("section", None, ("tensor", "replica"), None),
        P("section", None, ("tensor", "replica")),
        P("section", ("tensor", "replica"), None),
    )
    out_specs = (
        P("section", None, ("tensor", "replica"), None),
        P("section", None, ("tensor", "replica")),
        P("section", ("tensor", "replica"), None),
        P("section", "replica", None, "tensor"),
    )
    return jax.shard_map(body, mesh=mesh, in_specs=in_specs, out_specs=out_specs, check_vma=False)
```

```python
import jax
import jax.numpy as jnp
from jax import lax
from jax.sharding import PartitionSpec as P

gelu_scale = 0.7978845608
gelu_cubic = 0.044715
f32 = jnp.float32
bf16 = jnp.bfloat16


def gelu_pair(pre_gelu):
    inner = gelu_scale * (pre_gelu + gelu_cubic * pre_gelu * pre_gelu * pre_gelu)
    tanh_part = jnp.tanh(inner)
    gelu_value = 0.5 * pre_gelu * (1.0 + tanh_part)
    gelu_slope = 0.5 * (1.0 + tanh_part) + 0.5 * pre_gelu * (
        1.0 - tanh_part * tanh_part
    ) * gelu_scale * (1.0 + 3.0 * gelu_cubic * pre_gelu * pre_gelu)
    return (gelu_value, gelu_slope)


def dot(a, b, ca=1, cb=0):
    return lax.dot_general(a, b, (((ca,), (cb,)), ((), ())), preferred_element_type=f32)


def swap(x):
    return lax.ppermute(x, "replica", [(0, 1), (1, 0)])


def gather(chunk, axes="tensor"):
    count = lax.axis_size(axes)
    spread = jnp.broadcast_to(chunk[None], (count, *chunk.shape))
    return lax.all_to_all(spread, axes, 0, 0)


def body(pool_inputs, pool_mixed, crop_ids, incoming, loss_grads, w_proj, w_up, w_down):
    section = lax.axis_index("section")
    sections = lax.axis_size("section")
    replica = lax.axis_index("replica")
    parts = lax.axis_size("tensor")
    half = sections // 2
    first = replica == 0
    is_top = section == sections - 1
    ticks, rows = crop_ids.shape[1:]
    pool = pool_mixed.shape[1]
    width = pool_mixed.shape[2]
    units = w_down.shape[1]
    own_in = w_proj.shape[2]
    chunk_rows = incoming.shape[2]

    def by_replica(own, other):
        return jnp.where(first, own, other), jnp.where(first, other, own)

    def tied(*values):
        return lax.optimization_barrier(values)

    up_other = swap(w_up[0])
    down_other = swap(w_down[0])
    proj_other = swap(w_proj[0])

    chunk = incoming[0].T
    upstream = gather(chunk).reshape(width, rows)

    up = jnp.concatenate([w_up[0], up_other], axis=1)
    down = jnp.concatenate([w_down[0], down_other], axis=0)
    proj = jnp.concatenate(by_replica(w_proj[0], proj_other), axis=1).reshape(-1, width)

    places = jnp.arange(pool, dtype=jnp.int32)[:, None]
    pick = [(ids[None, :] == places).astype(bf16) for ids in crop_ids[0]]

    pre = dot(up, pool_mixed[0], 0, 1)
    value, slope = gelu_pair(pre)
    active = value.astype(bf16)
    high = slope.astype(bf16)
    low = (slope - high.astype(f32)).astype(bf16)

    decoder = jnp.where(section < half, 0.0, 1.0).astype(bf16)
    mask = jnp.stack([jnp.ones((), bf16), decoder])[:, None, None]
    saved = pool_inputs[0].transpose(1, 2, 0) * mask
    saved_first, saved_second = saved[:, :own_in], saved[:, own_in:]
    saved_own = jnp.where(first, saved_first, saved_second).reshape(-1, pool)
    saved_sent = jnp.where(first, saved_second, saved_first).reshape(-1, pool)
    ids_sent = jnp.broadcast_to(crop_ids[0, ticks - 1].astype(bf16)[None], (16, rows))
    mixed_sent = lax.dynamic_slice_in_dim(
        pool_mixed[0], lax.axis_index("tensor") * chunk_rows, chunk_rows, 1
    ).T
    side = jnp.concatenate([mixed_sent, saved_sent, active[units:], ids_sent], axis=0)

    def scatter(x, t):
        return dot(x, pick[t], 1, 1)

    def split(arrived):
        return (
            arrived[:, :chunk_rows].reshape(width, rows),
            arrived[:, chunk_rows:].reshape(width, pool),
        )

    seen, spread, early, seen_chunk, early_chunk = 0.0, 0.0, 0.0, 0.0, 0.0
    for t in range(ticks):
        last = t + 1 == ticks
        slope_now = dot(high, pick[t]) + dot(low, pick[t])
        hidden = (dot(down, upstream) * slope_now).astype(bf16)
        partial = dot(up, hidden).astype(bf16)
        sent = partial.reshape(parts, chunk_rows, rows)
        if last:
            rider = jnp.broadcast_to(seen_rider[None], (parts, chunk_rows, pool))
            sent = jnp.concatenate([sent, rider], axis=1)
        terms = lax.all_to_all(sent, "tensor", 0, 0)
        upstream_late, hidden_late, chunk_late, _ = tied(upstream, hidden, chunk, partial)
        seen = seen + scatter(upstream_late, t)
        spread = spread + scatter(hidden_late, t)
        seen_chunk = seen_chunk + scatter(chunk_late, t)
        if last:
            seen = seen.astype(bf16)
            spread = spread.astype(bf16)
            spread_other = swap(spread[units:])
            terms, seen_other = terms[:, :chunk_rows], terms[:, chunk_rows:]
            seen_other = seen_other.reshape(width, pool)
        mixed_chunk = (
            jnp.sum(terms.astype(f32), axis=0) + chunk.astype(f32)
        ).astype(bf16)
        if last:
            break
        early_chunk = early_chunk + scatter(mixed_chunk, t)
        mixed_grad = gather(mixed_chunk).reshape(width, rows)
        if t + 2 == ticks:
            early_rider = swap(early_chunk.astype(bf16))
            mixed_grad, early_rider = tied(mixed_grad, early_rider)
        early = early + scatter(mixed_grad, t)
        input_grad = dot(proj, mixed_grad).astype(bf16).reshape(2, chunk_rows, rows)
        above = lax.ppermute(
            input_grad[0], "section", [(i, i - 1) for i in range(1, sections)]
        )
        mirrored = lax.ppermute(
            input_grad[1],
            "section",
            [(i, sections - 1 - i) for i in range(half, sections)],
        )
        if t == 0:
            side, _ = tied(side, mixed_grad)
            side_other = swap(side)
        summed = (above.astype(f32) + mirrored.astype(f32)).astype(bf16)
        chunk = jnp.where(is_top, loss_grads[t].T, summed)
        if t == 1:
            upstream, mixed_other = split(
                gather(jnp.concatenate([chunk, side_other[:chunk_rows]], axis=0))
            )
        elif t + 2 == ticks:
            upstream, early_other = split(
                gather(jnp.concatenate([chunk, early_rider], axis=0))
            )
            seen_rider = swap((seen_chunk + scatter(chunk, t + 1)).astype(bf16))
        else:
            upstream = gather(chunk).reshape(width, rows)
            upstream, side_other = tied(upstream, side_other)

    both = gather(mixed_chunk, ("replica", "tensor")).reshape(2, width, rows)
    input_grad = jnp.where(first, dot(proj, both[0]), dot(proj, both[1]))
    input_grad = input_grad.astype(bf16).reshape(2, chunk_rows, rows)

    start = chunk_rows + saved_own.shape[0]
    saved_other = side_other[chunk_rows:start]
    active_other = side_other[start : start + units]
    ids_other = side_other[start + units].astype(jnp.int32)
    pick_other = (ids_other[None, :] == places).astype(bf16)
    last_own = dot(saved_own, pick[ticks - 1]).astype(bf16)
    last_other = dot(saved_other, pick_other).astype(bf16)
    grad_up = dot(pool_mixed[0], spread[:units], 0, 1) + dot(
        mixed_other, spread_other, 1, 1
    )
    grad_down = dot(
        jnp.concatenate([active[:units], active_other], axis=1),
        jnp.concatenate([seen, seen_other], axis=1),
        1,
        1,
    ).astype(bf16)
    grad_up = grad_up.astype(bf16)
    grad_proj = dot(
        jnp.concatenate(
            [saved_own, saved_other, *by_replica(last_own, last_other)], axis=1
        ),
        jnp.concatenate([early.astype(bf16), early_other, both[0], both[1]], axis=1),
        1,
        1,
    ).astype(bf16)
    return (
        grad_proj.reshape(1, 2, own_in, width),
        grad_up[None],
        grad_down[None],
        input_grad.transpose(2, 0, 1)[None],
    )


def solution(mesh):
    in_specs = (
        P("section", "replica", None, "tensor"),
        P("section", "replica", None),
        P("section", "replica", None),
        P("section", "replica", "tensor"),
        P(None, "replica", "tensor"),
        P("section", None, ("tensor", "replica"), None),
        P("section", None, ("tensor", "replica")),
        P("section", ("tensor", "replica"), None),
    )
    out_specs = (
        P("section", None, ("tensor", "replica"), None),
        P("section", None, ("tensor", "replica")),
        P("section", ("tensor", "replica"), None),
        P("section", "replica", None, "tensor"),
    )
    return jax.shard_map(body, mesh=mesh, in_specs=in_specs, out_specs=out_specs, check_vma=False)
```

```python
import jax
import jax.numpy as jnp
from jax import lax
from jax.sharding import PartitionSpec as P

gelu_scale = 0.7978845608
gelu_cubic = 0.044715
f32 = jnp.float32
bf16 = jnp.bfloat16


def gelu_pair(pre_gelu):
    inner = gelu_scale * (pre_gelu + gelu_cubic * pre_gelu * pre_gelu * pre_gelu)
    tanh_part = jnp.tanh(inner)
    gelu_value = 0.5 * pre_gelu * (1.0 + tanh_part)
    gelu_slope = 0.5 * (1.0 + tanh_part) + 0.5 * pre_gelu * (
        1.0 - tanh_part * tanh_part
    ) * gelu_scale * (1.0 + 3.0 * gelu_cubic * pre_gelu * pre_gelu)
    return (gelu_value, gelu_slope)


def dot(a, b, ca=1, cb=0):
    return lax.dot_general(a, b, (((ca,), (cb,)), ((), ())), preferred_element_type=f32)


def swap(x):
    return lax.ppermute(x, "replica", [(0, 1), (1, 0)])


def gather(chunk, axes="tensor"):
    count = lax.axis_size(axes)
    spread = jnp.broadcast_to(chunk[None], (count, *chunk.shape))
    return lax.all_to_all(spread, axes, 0, 0)


def body(pool_inputs, pool_mixed, crop_ids, incoming, loss_grads, w_proj, w_up, w_down):
    section = lax.axis_index("section")
    sections = lax.axis_size("section")
    replica = lax.axis_index("replica")
    parts = lax.axis_size("tensor")
    half = sections // 2
    first = replica == 0
    is_top = section == sections - 1
    ticks, rows = crop_ids.shape[1:]
    pool = pool_mixed.shape[1]
    width = pool_mixed.shape[2]
    units = w_down.shape[1]
    own_in = w_proj.shape[2]
    chunk_rows = incoming.shape[2]

    def by_replica(own, other):
        return jnp.where(first, own, other), jnp.where(first, other, own)

    def tied(*values):
        return lax.optimization_barrier(values)

    def pick_of(ids):
        places = jnp.arange(pool, dtype=jnp.int32)[:, None]
        return (ids[None, :] == places).astype(bf16)

    def other_of(pair):
        return jnp.where(first, pair[1], pair[0])

    up_other = swap(w_up[0])
    down_other = swap(w_down[0])
    proj_rows = 2 * own_in
    flat_inputs = pool_inputs[0].transpose(1, 2, 0).reshape(-1, width)
    ids_row = jnp.pad(crop_ids[0, ticks - 1].astype(bf16), (0, width - rows))
    ids_rows = jnp.broadcast_to(ids_row[None], (16, width))
    pairs = lax.all_gather(
        jnp.concatenate(
            [w_proj[0].reshape(proj_rows, width), pool_mixed[0], flat_inputs, ids_rows],
            axis=0,
        ),
        "replica",
    )
    proj = pairs[:, :proj_rows].reshape(2, 2, own_in, width).transpose(1, 0, 2, 3)
    proj = proj.reshape(-1, width)
    mixed_pair = pairs[:, proj_rows : proj_rows + pool]
    inputs_pair = pairs[:, proj_rows + pool : -16].reshape(2, 2, -1, pool)
    ids_pair = pairs[:, -1, :rows].astype(jnp.int32)

    chunk = incoming[0].T
    upstream = gather(chunk).reshape(width, rows)

    up = jnp.concatenate([w_up[0], up_other], axis=1)
    down = jnp.concatenate([w_down[0], down_other], axis=0)
    pick = [pick_of(ids) for ids in crop_ids[0]]

    def hidden_parts(weight, mixed):
        value, slope = gelu_pair(dot(weight, mixed, 0, 1))
        high = slope.astype(bf16)
        low = (slope - high.astype(f32)).astype(bf16)
        return value.astype(bf16), high, low

    active, high, low = hidden_parts(up, pool_mixed[0])

    def scatter(x, t):
        return dot(x, pick[t], 1, 1)

    seen, spread, early = 0.0, 0.0, 0.0
    for t in range(ticks):
        last = t + 1 == ticks
        slope_now = dot(high, pick[t]) + dot(low, pick[t])
        if last:
            backs = dot(down, upstreams[0]), dot(down, upstreams[1])
            back = jnp.where(first, *backs)
        else:
            back = dot(down, upstream)
        hidden = (back * slope_now).astype(bf16)
        partial = dot(up, hidden).astype(bf16)
        terms = lax.all_to_all(partial.reshape(parts, chunk_rows, rows), "tensor", 0, 0)
        mixed_chunk = (
            jnp.sum(terms.astype(f32), axis=0) + chunk.astype(f32)
        ).astype(bf16)
        if last:
            break
        upstream_late, hidden_late, _ = tied(upstream, hidden, partial)
        seen = seen + scatter(upstream_late, t)
        spread = spread + scatter(hidden_late, t)
        mixed_grad = gather(mixed_chunk).reshape(width, rows)
        early = early + scatter(mixed_grad, t)
        input_grad = dot(proj, mixed_grad).astype(bf16).reshape(2, chunk_rows, rows)
        above = lax.ppermute(
            input_grad[0], "section", [(i, i - 1) for i in range(1, sections)]
        )
        mirrored = lax.ppermute(
            input_grad[1],
            "section",
            [(i, sections - 1 - i) for i in range(half, sections)],
        )
        summed = (above.astype(f32) + mirrored.astype(f32)).astype(bf16)
        chunk = jnp.where(is_top, loss_grads[t].T, summed)
        if t + 2 == ticks:
            factors = jnp.concatenate([seen, early, spread[units:]], axis=0)
            factors = lax.all_gather(factors.astype(bf16), "replica")
            upstreams = gather(chunk, ("replica", "tensor")).reshape(2, width, rows)
        else:
            upstream = gather(chunk).reshape(width, rows)

    mixed_grads = gather(mixed_chunk, ("replica", "tensor")).reshape(2, width, rows)
    input_grad = jnp.where(first, dot(proj, mixed_grads[0]), dot(proj, mixed_grads[1]))
    input_grad = input_grad.astype(bf16).reshape(2, chunk_rows, rows)

    pick_other = pick_of(other_of(ids_pair))
    mixed_other = other_of(mixed_pair)
    active_other, high, low = hidden_parts(w_up[0], mixed_other)
    slope_other = dot(high, pick_other) + dot(low, pick_other)
    back_other = jnp.where(first, backs[1], backs[0])[:units]
    hidden_other = (back_other * slope_other).astype(bf16)
    spread_own = spread[:units] + scatter(hidden[:units], ticks - 1)
    spread_other = other_of(factors[:, 2 * width :]).astype(f32)
    spread_other = spread_other + dot(hidden_other, pick_other, 1, 1)
    grad_up = dot(
        jnp.concatenate([pool_mixed[0], mixed_other], axis=0),
        jnp.concatenate([spread_own, spread_other], axis=1).astype(bf16),
        0,
        1,
    ).astype(bf16)

    picks = by_replica(pick[ticks - 1], pick_other)
    actives = by_replica(active[:units], active_other)
    seens = [
        (factors[r, :width].astype(f32) + dot(upstreams[r], picks[r], 1, 1)).astype(bf16)
        for r in range(2)
    ]
    grad_down = dot(
        jnp.concatenate(actives, axis=1), jnp.concatenate(seens, axis=1), 1, 1
    ).astype(bf16)

    decoder = jnp.where(section < half, 0.0, 1.0).astype(bf16)
    mask = jnp.stack([jnp.ones((), bf16), decoder])[:, None, None]
    saved = inputs_pair * mask
    saved = jnp.where(first, saved[:, :, :own_in], saved[:, :, own_in:])
    saved = saved.reshape(2, 2 * own_in, pool)
    lasts = [dot(saved[r], picks[r]).astype(bf16) for r in range(2)]
    grad_proj = dot(
        jnp.concatenate([saved[0], saved[1], *lasts], axis=1),
        jnp.concatenate(
            [factors[0, width : 2 * width], factors[1, width : 2 * width], *mixed_grads],
            axis=1,
        ),
        1,
        1,
    ).astype(bf16)
    return (
        grad_proj.reshape(1, 2, own_in, width),
        grad_up[None],
        grad_down[None],
        input_grad.transpose(2, 0, 1)[None],
    )


def solution(mesh):
    in_specs = (
        P("section", "replica", None, "tensor"),
        P("section", "replica", None),
        P("section", "replica", None),
        P("section", "replica", "tensor"),
        P(None, "replica", "tensor"),
        P("section", None, ("tensor", "replica"), None),
        P("section", None, ("tensor", "replica")),
        P("section", ("tensor", "replica"), None),
    )
    out_specs = (
        P("section", None, ("tensor", "replica"), None),
        P("section", None, ("tensor", "replica")),
        P("section", ("tensor", "replica"), None),
        P("section", "replica", None, "tensor"),
    )
    return jax.shard_map(body, mesh=mesh, in_specs=in_specs, out_specs=out_specs, check_vma=False)
```

```python
import jax
import jax.numpy as jnp
from jax import lax
from jax.sharding import PartitionSpec as P

gelu_scale = 0.7978845608
gelu_cubic = 0.044715
f32 = jnp.float32
bf16 = jnp.bfloat16


def gelu_pair(pre_gelu):
    inner = gelu_scale * (pre_gelu + gelu_cubic * pre_gelu * pre_gelu * pre_gelu)
    tanh_part = jnp.tanh(inner)
    gelu_value = 0.5 * pre_gelu * (1.0 + tanh_part)
    gelu_slope = 0.5 * (1.0 + tanh_part) + 0.5 * pre_gelu * (
        1.0 - tanh_part * tanh_part
    ) * gelu_scale * (1.0 + 3.0 * gelu_cubic * pre_gelu * pre_gelu)
    return (gelu_value, gelu_slope)


def dot(a, b, ca=1, cb=0):
    return lax.dot_general(a, b, (((ca,), (cb,)), ((), ())), preferred_element_type=f32)


def swap(x):
    return lax.ppermute(x, "replica", [(0, 1), (1, 0)])


def gather(chunk, axes="tensor"):
    count = lax.axis_size(axes)
    spread = jnp.broadcast_to(chunk[None], (count, *chunk.shape))
    return lax.all_to_all(spread, axes, 0, 0)


def body(pool_inputs, pool_mixed, crop_ids, incoming, loss_grads, w_proj, w_up, w_down):
    section = lax.axis_index("section")
    sections = lax.axis_size("section")
    replica = lax.axis_index("replica")
    parts = lax.axis_size("tensor")
    half = sections // 2
    first = replica == 0
    is_top = section == sections - 1
    ticks, rows = crop_ids.shape[1:]
    pool = pool_mixed.shape[1]
    width = pool_mixed.shape[2]
    units = w_down.shape[1]
    own_in = w_proj.shape[2]
    chunk_rows = incoming.shape[2]

    def by_replica(own, other):
        return jnp.where(first, own, other), jnp.where(first, other, own)

    def tied(*values):
        return lax.optimization_barrier(values)

    up_other = swap(w_up[0])
    down_other = swap(w_down[0])
    chunk = incoming[0].T
    upstream = gather(chunk).reshape(width, rows)
    upstream, proj_own = tied(upstream, w_proj[0])
    proj_other = swap(proj_own)

    (up,) = tied(jnp.concatenate([w_up[0], up_other], axis=1))
    (down,) = tied(jnp.concatenate([w_down[0], down_other], axis=0))
    proj = jnp.concatenate(by_replica(proj_own, proj_other), axis=1).reshape(-1, width)

    places = jnp.arange(pool, dtype=jnp.int32)[:, None]
    pick = [(ids[None, :] == places).astype(bf16) for ids in crop_ids[0]]

    pre = dot(up, pool_mixed[0], 0, 1)
    value, slope = gelu_pair(pre)
    active = value.astype(bf16)
    high = slope.astype(bf16)
    low = (slope - high.astype(f32)).astype(bf16)

    decoder = jnp.where(section < half, 0.0, 1.0).astype(bf16)
    mask = jnp.stack([jnp.ones((), bf16), decoder])[:, None, None]
    saved = pool_inputs[0].transpose(1, 2, 0) * mask
    saved_first, saved_second = saved[:, :own_in], saved[:, own_in:]
    saved_own = jnp.where(first, saved_first, saved_second).reshape(-1, pool)
    saved_sent = jnp.where(first, saved_second, saved_first).reshape(-1, pool)
    ids_sent = jnp.broadcast_to(crop_ids[0, ticks - 1].astype(bf16)[None], (16, rows))
    small = jnp.concatenate([saved_sent, active[units:], ids_sent], axis=0)

    seen, spread, early = 0.0, 0.0, 0.0
    for t in range(ticks):
        slope_now = dot(high, pick[t]) + dot(low, pick[t])
        hidden = (dot(down, upstream) * slope_now).astype(bf16)
        partial = dot(up, hidden).astype(bf16)
        terms = lax.all_to_all(partial.reshape(parts, chunk_rows, rows), "tensor", 0, 0)
        upstream_late, hidden_late, _ = tied(upstream, hidden, partial)
        seen = seen + dot(upstream_late, pick[t], 1, 1)
        spread = spread + dot(hidden_late, pick[t], 1, 1)
        if t + 1 == ticks:
            seen = seen.astype(bf16)
            seen_other = swap(seen)
            spread = spread.astype(bf16)
            spread_other = swap(spread[units:])
        mixed_chunk = (
            jnp.sum(terms.astype(f32), axis=0) + chunk.astype(f32)
        ).astype(bf16)
        if t + 1 < ticks:
            mixed_grad = gather(mixed_chunk).reshape(width, rows)
            early = early + dot(mixed_grad, pick[t], 1, 1)
            input_grad = dot(proj, mixed_grad).astype(bf16).reshape(2, chunk_rows, rows)
            above = lax.ppermute(
                input_grad[0], "section", [(i, i - 1) for i in range(1, sections)]
            )
            mirrored = lax.ppermute(
                input_grad[1],
                "section",
                [(i, sections - 1 - i) for i in range(half, sections)],
            )
            if t == 0:
                mixed_own, _ = tied(pool_mixed[0], mixed_grad)
                sent = swap(mixed_own)
            elif t == 1:
                small, _ = tied(small, mixed_grad)
                sent = swap(small)
            else:
                early = early.astype(bf16)
                sent = swap(early)
            summed = (above.astype(f32) + mirrored.astype(f32)).astype(bf16)
            chunk = jnp.where(is_top, loss_grads[t].T, summed)
            upstream = gather(chunk).reshape(width, rows)
            upstream, sent = tied(upstream, sent)
            if t == 0:
                mixed_other = sent
            elif t == 1:
                count = saved_own.shape[0]
                saved_other = sent[:count]
                active_other = sent[count : count + units]
                ids_other = sent[count + units].astype(jnp.int32)
                pick_other = (ids_other[None, :] == places).astype(bf16)
                last_own = dot(saved_own, pick[ticks - 1]).astype(bf16)
                last_other = dot(saved_other, pick_other).astype(bf16)
            else:
                early_other = sent
        else:
            both = gather(mixed_chunk, ("replica", "tensor")).reshape(2, width, rows)
            input_grad = jnp.where(first, dot(proj, both[0]), dot(proj, both[1]))
            input_grad = input_grad.astype(bf16).reshape(2, chunk_rows, rows)

    grad_up = dot(
        jnp.concatenate([pool_mixed[0], mixed_other], axis=0),
        jnp.concatenate([spread[:units], spread_other], axis=1),
        0,
        1,
    ).astype(bf16)
    grad_down = dot(
        jnp.concatenate([active[:units], active_other], axis=1),
        jnp.concatenate([seen, seen_other], axis=1),
        1,
        1,
    ).astype(bf16)
    grad_proj = dot(
        jnp.concatenate(
            [saved_own, saved_other, *by_replica(last_own, last_other)], axis=1
        ),
        jnp.concatenate([early, early_other, both[0], both[1]], axis=1),
        1,
        1,
    ).astype(bf16)
    return (
        grad_proj.reshape(1, 2, own_in, width),
        grad_up[None],
        grad_down[None],
        input_grad.transpose(2, 0, 1)[None],
    )


def solution(mesh):
    in_specs = (
        P("section", "replica", None, "tensor"),
        P("section", "replica", None),
        P("section", "replica", None),
        P("section", "replica", "tensor"),
        P(None, "replica", "tensor"),
        P("section", None, ("tensor", "replica"), None),
        P("section", None, ("tensor", "replica")),
        P("section", ("tensor", "replica"), None),
    )
    out_specs = (
        P("section", None, ("tensor", "replica"), None),
        P("section", None, ("tensor", "replica")),
        P("section", ("tensor", "replica"), None),
        P("section", "replica", None, "tensor"),
    )
    return jax.shard_map(body, mesh=mesh, in_specs=in_specs, out_specs=out_specs, check_vma=False)
```

```python
import jax
import jax.numpy as jnp
from jax import lax
from jax.sharding import PartitionSpec as P

gelu_scale = 0.7978845608
gelu_cubic = 0.044715
f32 = jnp.float32
bf16 = jnp.bfloat16


def gelu_pair(pre_gelu):
    inner = gelu_scale * (pre_gelu + gelu_cubic * pre_gelu * pre_gelu * pre_gelu)
    tanh_part = jnp.tanh(inner)
    gelu_value = 0.5 * pre_gelu * (1.0 + tanh_part)
    gelu_slope = 0.5 * (1.0 + tanh_part) + 0.5 * pre_gelu * (
        1.0 - tanh_part * tanh_part
    ) * gelu_scale * (1.0 + 3.0 * gelu_cubic * pre_gelu * pre_gelu)
    return (gelu_value, gelu_slope)


def dot(a, b, ca=1, cb=0):
    return lax.dot_general(a, b, (((ca,), (cb,)), ((), ())), preferred_element_type=f32)


def swap(x):
    return lax.ppermute(x, "replica", [(0, 1), (1, 0)])


def tied(*values):
    return lax.optimization_barrier(values)


def gather(chunk, axes="tensor"):
    count = lax.axis_size(axes)
    spread = jnp.broadcast_to(chunk[None], (count, *chunk.shape))
    return lax.all_to_all(spread, axes, 0, 0)


def body(pool_inputs, pool_mixed, crop_ids, incoming, loss_grads, w_proj, w_up, w_down):
    section = lax.axis_index("section")
    sections = lax.axis_size("section")
    replica = lax.axis_index("replica")
    parts = lax.axis_size("tensor")
    half = sections // 2
    first = replica == 0
    is_top = section == sections - 1
    ticks, rows = crop_ids.shape[1:]
    pool = pool_mixed.shape[1]
    width = pool_mixed.shape[2]
    units = w_down.shape[1]
    own_in = w_proj.shape[2]
    chunk_rows = incoming.shape[2]

    def by_replica(own, other):
        return jnp.where(first, own, other), jnp.where(first, other, own)

    up_other = swap(w_up[0])
    down_other = swap(w_down[0])
    proj_other = swap(w_proj[0])
    mixed_other = swap(pool_mixed[0])
    ids_other = swap(crop_ids[0, ticks - 1])

    chunk = incoming[0].T
    upstream = gather(chunk).reshape(width, rows)

    up = jnp.concatenate([w_up[0], up_other], axis=1)
    down = jnp.concatenate([w_down[0], down_other], axis=0)
    proj = jnp.concatenate(by_replica(w_proj[0], proj_other), axis=1).reshape(-1, width)

    places = jnp.arange(pool, dtype=jnp.int32)[:, None]
    pick = (crop_ids[0].reshape(1, -1) == places).astype(bf16)
    pick_other = (ids_other[None, :] == places).astype(bf16)

    def picked(t):
        return pick[:, t * rows : (t + 1) * rows]

    pre = dot(up, pool_mixed[0], 0, 1)
    value, slope = gelu_pair(pre)
    active = value.astype(bf16)
    high = slope.astype(bf16)
    low = (slope - high.astype(f32)).astype(bf16)
    slopes = dot(high, pick) + dot(low, pick)

    decoder = jnp.where(section < half, 0.0, 1.0).astype(bf16)
    mask = jnp.stack([jnp.ones((), bf16), decoder])[:, None, None]
    saved = pool_inputs[0].transpose(1, 2, 0) * mask
    saved_first, saved_second = saved[:, :own_in], saved[:, own_in:]
    saved_own = jnp.where(first, saved_first, saved_second).reshape(-1, pool)
    saved_sent = jnp.where(first, saved_second, saved_first).reshape(-1, pool)
    saved_other = swap(saved_sent)
    last_own = dot(saved_own, picked(ticks - 1)).astype(bf16)
    last_other = dot(saved_other, pick_other).astype(bf16)

    hiddens, grads, upstreams = [], [], []
    for t in range(ticks):
        upstreams.append(upstream)
        slope_now = slopes[:, t * rows : (t + 1) * rows]
        hidden = (dot(down, upstream) * slope_now).astype(bf16)
        hiddens.append(hidden)
        partial = dot(up, hidden).astype(bf16)
        if t + 1 == ticks:
            seen = dot(jnp.concatenate(upstreams, axis=1), pick, 1, 1).astype(bf16)
            seen_other = swap(seen)
        terms = lax.all_to_all(partial.reshape(parts, chunk_rows, rows), "tensor", 0, 0)
        mixed_chunk = (
            jnp.sum(terms.astype(f32), axis=0) + chunk.astype(f32)
        ).astype(bf16)
        if t + 1 < ticks:
            mixed_grad = gather(mixed_chunk).reshape(width, rows)
            grads.append(mixed_grad)
            skip_grad = dot(proj[chunk_rows:], mixed_grad).astype(bf16)
            mirrored = lax.ppermute(
                skip_grad,
                "section",
                [(i, sections - 1 - i) for i in range(half, sections)],
            )
            later_grad, _ = tied(mixed_grad, skip_grad)
            above = lax.ppermute(
                dot(proj[:chunk_rows], later_grad).astype(bf16),
                "section",
                [(i, i - 1) for i in range(1, sections)],
            )
            if t + 3 == ticks:
                active_sent, _ = tied(active[units:], skip_grad)
                sent = swap(active_sent)
            elif t + 2 == ticks:
                early = dot(jnp.concatenate(grads, axis=1), pick[:, : (t + 1) * rows], 1, 1)
                early = early.astype(bf16)
                sent = swap(early)
            summed = (above.astype(f32) + mirrored.astype(f32)).astype(bf16)
            chunk = jnp.where(is_top, loss_grads[t].T, summed)
            upstream = gather(chunk).reshape(width, rows)
            if t + 3 == ticks:
                upstream, active_other = tied(upstream, sent)
            elif t + 2 == ticks:
                upstream, early_other = tied(upstream, sent)
        else:
            spread = dot(jnp.concatenate(hiddens, axis=1), pick, 1, 1).astype(bf16)
            spread_other = swap(spread[units:])
            both = gather(mixed_chunk, ("replica", "tensor")).reshape(2, width, rows)
            mixed_grad = jnp.where(first, both[0], both[1])
            input_grad = dot(proj, mixed_grad).astype(bf16).reshape(2, chunk_rows, rows)

    grad_up = dot(
        jnp.concatenate([pool_mixed[0], mixed_other], axis=0),
        jnp.concatenate([spread[:units], spread_other], axis=1),
        0,
        1,
    ).astype(bf16)
    grad_down = dot(
        jnp.concatenate([active[:units], active_other], axis=1),
        jnp.concatenate([seen, seen_other], axis=1),
        1,
        1,
    ).astype(bf16)
    grad_proj = dot(
        jnp.concatenate(
            [saved_own, saved_other, *by_replica(last_own, last_other)], axis=1
        ),
        jnp.concatenate([early, early_other, both[0], both[1]], axis=1),
        1,
        1,
    ).astype(bf16)
    return (
        grad_proj.reshape(1, 2, own_in, width),
        grad_up[None],
        grad_down[None],
        input_grad.transpose(2, 0, 1)[None],
    )


def solution(mesh):
    in_specs = (
        P("section", "replica", None, "tensor"),
        P("section", "replica", None),
        P("section", "replica", None),
        P("section", "replica", "tensor"),
        P(None, "replica", "tensor"),
        P("section", None, ("tensor", "replica"), None),
        P("section", None, ("tensor", "replica")),
        P("section", ("tensor", "replica"), None),
    )
    out_specs = (
        P("section", None, ("tensor", "replica"), None),
        P("section", None, ("tensor", "replica")),
        P("section", ("tensor", "replica"), None),
        P("section", "replica", None, "tensor"),
    )
    return jax.shard_map(body, mesh=mesh, in_specs=in_specs, out_specs=out_specs, check_vma=False)
```

```python
import jax
import jax.numpy as jnp
from jax import lax
from jax.sharding import PartitionSpec as P

gelu_scale = 0.7978845608
gelu_cubic = 0.044715
f32 = jnp.float32
bf16 = jnp.bfloat16


def gelu_pair(pre_gelu):
    inner = gelu_scale * (pre_gelu + gelu_cubic * pre_gelu * pre_gelu * pre_gelu)
    tanh_part = jnp.tanh(inner)
    gelu_value = 0.5 * pre_gelu * (1.0 + tanh_part)
    gelu_slope = 0.5 * (1.0 + tanh_part) + 0.5 * pre_gelu * (
        1.0 - tanh_part * tanh_part
    ) * gelu_scale * (1.0 + 3.0 * gelu_cubic * pre_gelu * pre_gelu)
    return (gelu_value, gelu_slope)


def dot(a, b, ca=1, cb=0):
    return lax.dot_general(a, b, (((ca,), (cb,)), ((), ())), preferred_element_type=f32)


def swap(x):
    return lax.ppermute(x, "replica", [(0, 1), (1, 0)])


def tied(*values):
    return lax.optimization_barrier(values)


def gather(chunk, axes="tensor"):
    count = lax.axis_size(axes)
    spread = jnp.broadcast_to(chunk[None], (count, *chunk.shape))
    return lax.all_to_all(spread, axes, 0, 0)


def body(pool_inputs, pool_mixed, crop_ids, incoming, loss_grads, w_proj, w_up, w_down):
    section = lax.axis_index("section")
    sections = lax.axis_size("section")
    replica = lax.axis_index("replica")
    parts = lax.axis_size("tensor")
    half = sections // 2
    first = replica == 0
    is_top = section == sections - 1
    ticks, rows = crop_ids.shape[1:]
    pool = pool_mixed.shape[1]
    width = pool_mixed.shape[2]
    units = w_down.shape[1]
    own_in = w_proj.shape[2]
    chunk_rows = incoming.shape[2]

    def by_replica(own, other):
        return jnp.where(first, own, other), jnp.where(first, other, own)

    up_other = swap(w_up[0])
    down_other = swap(w_down[0])
    proj_other = swap(w_proj[0])
    mixed_other = swap(pool_mixed[0])
    ids_other = swap(crop_ids[0, ticks - 1])

    chunk = incoming[0].T
    upstream = gather(chunk).reshape(width, rows)

    up = jnp.concatenate([w_up[0], up_other], axis=1)
    (down,) = tied(jnp.concatenate([w_down[0], down_other], axis=0))
    proj = jnp.concatenate(by_replica(w_proj[0], proj_other), axis=1).reshape(-1, width)

    places = jnp.arange(pool, dtype=jnp.int32)[:, None]
    pick = (crop_ids[0].reshape(1, -1) == places).astype(bf16)
    pick_other = (ids_other[None, :] == places).astype(bf16)

    def picked(t):
        return pick[:, t * rows : (t + 1) * rows]

    pre = dot(up, pool_mixed[0], 0, 1)
    value, slope = gelu_pair(pre)
    active = value.astype(bf16)
    high = slope.astype(bf16)
    low = (slope - high.astype(f32)).astype(bf16)
    slopes = dot(high, pick) + dot(low, pick)

    decoder = jnp.where(section < half, 0.0, 1.0).astype(bf16)
    mask = jnp.stack([jnp.ones((), bf16), decoder])[:, None, None]
    saved = pool_inputs[0].transpose(1, 2, 0) * mask
    saved_first, saved_second = saved[:, :own_in], saved[:, own_in:]
    saved_own = jnp.where(first, saved_first, saved_second).reshape(-1, pool)
    saved_sent = jnp.where(first, saved_second, saved_first).reshape(-1, pool)
    saved_other = swap(saved_sent)
    last_own = dot(saved_own, picked(ticks - 1)).astype(bf16)
    last_other = dot(saved_other, pick_other).astype(bf16)

    hiddens, grads, upstreams = [], [], []
    for t in range(ticks):
        upstreams.append(upstream)
        slope_now = slopes[:, t * rows : (t + 1) * rows]
        hidden = (dot(down, upstream) * slope_now).astype(bf16)
        hiddens.append(hidden)
        partial = dot(up, hidden).astype(bf16)
        if t + 1 == ticks:
            seen = dot(jnp.concatenate(upstreams, axis=1), pick, 1, 1).astype(bf16)
            seen_other = swap(seen)
        terms = lax.all_to_all(partial.reshape(parts, chunk_rows, rows), "tensor", 0, 0)
        mixed_chunk = (
            jnp.sum(terms.astype(f32), axis=0) + chunk.astype(f32)
        ).astype(bf16)
        if t + 1 < ticks:
            mixed_grad = gather(mixed_chunk).reshape(width, rows)
            grads.append(mixed_grad)
            skip_grad = dot(proj[chunk_rows:], mixed_grad).astype(bf16)
            mirrored = lax.ppermute(
                skip_grad,
                "section",
                [(i, sections - 1 - i) for i in range(half, sections)],
            )
            later_grad, _ = tied(mixed_grad, skip_grad)
            above = lax.ppermute(
                dot(proj[:chunk_rows], later_grad).astype(bf16),
                "section",
                [(i, i - 1) for i in range(1, sections)],
            )
            if t + 3 == ticks:
                active_sent, _ = tied(active[units:], skip_grad)
                sent = swap(active_sent)
            elif t + 2 == ticks:
                early = dot(jnp.concatenate(grads, axis=1), pick[:, : (t + 1) * rows], 1, 1)
                early = early.astype(bf16)
                sent = swap(early)
            summed = (above.astype(f32) + mirrored.astype(f32)).astype(bf16)
            chunk = jnp.where(is_top, loss_grads[t].T, summed)
            upstream = gather(chunk).reshape(width, rows)
            if t + 3 == ticks:
                upstream, active_other = tied(upstream, sent)
            elif t + 2 == ticks:
                upstream, early_other = tied(upstream, sent)
        else:
            spread = dot(jnp.concatenate(hiddens, axis=1), pick, 1, 1).astype(bf16)
            spread_other = swap(spread[units:])
            both = gather(mixed_chunk, ("replica", "tensor")).reshape(2, width, rows)
            input_grad = jnp.where(first, dot(proj, both[0]), dot(proj, both[1]))
            input_grad = input_grad.astype(bf16).reshape(2, chunk_rows, rows)

    grad_up = dot(
        jnp.concatenate([pool_mixed[0], mixed_other], axis=0),
        jnp.concatenate([spread[:units], spread_other], axis=1),
        0,
        1,
    ).astype(bf16)
    grad_down = dot(
        jnp.concatenate([active[:units], active_other], axis=1),
        jnp.concatenate([seen, seen_other], axis=1),
        1,
        1,
    ).astype(bf16)
    grad_proj = dot(
        jnp.concatenate(
            [saved_own, saved_other, *by_replica(last_own, last_other)], axis=1
        ),
        jnp.concatenate([early, early_other, both[0], both[1]], axis=1),
        1,
        1,
    ).astype(bf16)
    return (
        grad_proj.reshape(1, 2, own_in, width),
        grad_up[None],
        grad_down[None],
        input_grad.transpose(2, 0, 1)[None],
    )


def solution(mesh):
    in_specs = (
        P("section", "replica", None, "tensor"),
        P("section", "replica", None),
        P("section", "replica", None),
        P("section", "replica", "tensor"),
        P(None, "replica", "tensor"),
        P("section", None, ("tensor", "replica"), None),
        P("section", None, ("tensor", "replica")),
        P("section", ("tensor", "replica"), None),
    )
    out_specs = (
        P("section", None, ("tensor", "replica"), None),
        P("section", None, ("tensor", "replica")),
        P("section", ("tensor", "replica"), None),
        P("section", "replica", None, "tensor"),
    )
    return jax.shard_map(body, mesh=mesh, in_specs=in_specs, out_specs=out_specs, check_vma=False)
```

```python
import jax
import jax.numpy as jnp
from jax import lax
from jax.sharding import PartitionSpec as P

gelu_scale = 0.7978845608
gelu_cubic = 0.044715
f32 = jnp.float32
bf16 = jnp.bfloat16


def gelu_pair(pre_gelu):
    inner = gelu_scale * (pre_gelu + gelu_cubic * pre_gelu * pre_gelu * pre_gelu)
    tanh_part = jnp.tanh(inner)
    gelu_value = 0.5 * pre_gelu * (1.0 + tanh_part)
    gelu_slope = 0.5 * (1.0 + tanh_part) + 0.5 * pre_gelu * (
        1.0 - tanh_part * tanh_part
    ) * gelu_scale * (1.0 + 3.0 * gelu_cubic * pre_gelu * pre_gelu)
    return (gelu_value, gelu_slope)


def dot(a, b, ca=1, cb=0):
    return lax.dot_general(a, b, (((ca,), (cb,)), ((), ())), preferred_element_type=f32)


def swap(x):
    return lax.ppermute(x, "replica", [(0, 1), (1, 0)])


def tied(*values):
    return lax.optimization_barrier(values)


def gather(chunk, axes="tensor"):
    count = lax.axis_size(axes)
    spread = jnp.broadcast_to(chunk[None], (count, *chunk.shape))
    return lax.all_to_all(spread, axes, 0, 0)


def body(pool_inputs, pool_mixed, crop_ids, incoming, loss_grads, w_proj, w_up, w_down):
    section = lax.axis_index("section")
    sections = lax.axis_size("section")
    replica = lax.axis_index("replica")
    parts = lax.axis_size("tensor")
    half = sections // 2
    first = replica == 0
    is_top = section == sections - 1
    ticks, rows = crop_ids.shape[1:]
    pool = pool_mixed.shape[1]
    width = pool_mixed.shape[2]
    units = w_down.shape[1]
    own_in = w_proj.shape[2]
    chunk_rows = incoming.shape[2]

    def by_replica(own, other):
        return jnp.where(first, own, other), jnp.where(first, other, own)

    up_other = swap(w_up[0])
    down_other = swap(w_down[0])
    proj_other = swap(w_proj[0])

    chunk = incoming[0].T
    upstream = gather(chunk).reshape(width, rows)

    up = jnp.concatenate([w_up[0], up_other], axis=1)
    proj = jnp.concatenate(by_replica(w_proj[0], proj_other), axis=1).reshape(-1, width)

    places = jnp.arange(pool, dtype=jnp.int32)[:, None]
    pick = (crop_ids[0].reshape(1, -1) == places).astype(bf16)

    def picked(t):
        return pick[:, t * rows : (t + 1) * rows]

    pre = dot(up, pool_mixed[0], 0, 1)
    value, slope = gelu_pair(pre)
    active = value.astype(bf16)
    high = slope.astype(bf16)
    low = (slope - high.astype(f32)).astype(bf16)
    slopes = dot(high, pick) + dot(low, pick)
    down_own, down_other, slopes = tied(w_down[0], down_other, slopes)
    (down,) = tied(jnp.concatenate([down_own, down_other], axis=0))

    def small_of(inputs, active_sent, ids_sent):
        decoder = jnp.where(section < half, 0.0, 1.0).astype(bf16)
        mask = jnp.stack([jnp.ones((), bf16), decoder])[:, None, None]
        saved = inputs.transpose(1, 2, 0) * mask
        saved_first, saved_second = saved[:, :own_in], saved[:, own_in:]
        saved_own = jnp.where(first, saved_first, saved_second).reshape(-1, pool)
        saved_sent = jnp.where(first, saved_second, saved_first).reshape(-1, pool)
        ids = jnp.broadcast_to(ids_sent.astype(bf16)[None], (16, rows))
        return saved_own, jnp.concatenate([saved_sent, active_sent, ids], axis=0)

    hiddens, grads, upstreams = [], [], []
    for t in range(ticks):
        upstreams.append(upstream)
        slope_now = slopes[:, t * rows : (t + 1) * rows]
        hidden = (dot(down, upstream) * slope_now).astype(bf16)
        hiddens.append(hidden)
        partial = dot(up, hidden).astype(bf16)
        if t + 1 == ticks:
            upstreams[-1], _ = tied(upstream, partial)
            seen = dot(jnp.concatenate(upstreams, axis=1), pick, 1, 1).astype(bf16)
            seen_other = swap(seen)
        terms = lax.all_to_all(partial.reshape(parts, chunk_rows, rows), "tensor", 0, 0)
        mixed_chunk = (
            jnp.sum(terms.astype(f32), axis=0) + chunk.astype(f32)
        ).astype(bf16)
        if t + 1 < ticks:
            mixed_grad = gather(mixed_chunk).reshape(width, rows)
            grads.append(mixed_grad)
            skip_grad = dot(proj[chunk_rows:], mixed_grad).astype(bf16)
            mirrored = lax.ppermute(
                skip_grad,
                "section",
                [(i, sections - 1 - i) for i in range(half, sections)],
            )
            later_grad, _ = tied(mixed_grad, skip_grad)
            above = lax.ppermute(
                dot(proj[:chunk_rows], later_grad).astype(bf16),
                "section",
                [(i, i - 1) for i in range(1, sections)],
            )
            if t == 0:
                mixed_sent, _ = tied(pool_mixed[0], skip_grad)
                sent = swap(mixed_sent)
            elif t + 3 == ticks:
                inputs, active_late, ids_late, _ = tied(
                    pool_inputs[0], active, crop_ids, skip_grad
                )
                saved_own, small = small_of(
                    inputs, active_late[units:], ids_late[0, ticks - 1]
                )
                small_other = swap(small)
            elif t + 2 == ticks:
                ids_late, _ = tied(crop_ids, skip_grad)
                picks = (ids_late[0, : t + 1].reshape(1, -1) == places).astype(bf16)
                early = dot(jnp.concatenate(grads, axis=1), picks, 1, 1)
                early = early.astype(bf16)
                sent = swap(early)
            summed = (above.astype(f32) + mirrored.astype(f32)).astype(bf16)
            chunk = jnp.where(is_top, loss_grads[t].T, summed)
            if t + 3 == ticks:
                chunk, small_other = tied(chunk, small_other)
            upstream = gather(chunk).reshape(width, rows)
            if t == 0:
                upstream, mixed_other = tied(upstream, sent)
            elif t + 2 == ticks:
                upstream, early_other = tied(upstream, sent)
                upstream, saved_own, small_other = tied(upstream, saved_own, small_other)
                count = saved_own.shape[0]
                saved_other = small_other[:count]
                active_other = small_other[count : count + units]
                ids_other = small_other[count + units].astype(jnp.int32)
                pick_other = (ids_other[None, :] == places).astype(bf16)
                last_own = dot(saved_own, picked(ticks - 1)).astype(bf16)
                last_other = dot(saved_other, pick_other).astype(bf16)
        else:
            spread = dot(jnp.concatenate(hiddens, axis=1), pick, 1, 1).astype(bf16)
            spread_other = swap(spread[units:])
            both = gather(mixed_chunk, ("replica", "tensor")).reshape(2, width, rows)
            input_grad = jnp.where(first, dot(proj, both[0]), dot(proj, both[1]))
            input_grad = input_grad.astype(bf16).reshape(2, chunk_rows, rows)

    grad_up = dot(
        jnp.concatenate([pool_mixed[0], mixed_other], axis=0),
        jnp.concatenate([spread[:units], spread_other], axis=1),
        0,
        1,
    ).astype(bf16)
    grad_down = dot(
        jnp.concatenate([active[:units], active_other], axis=1),
        jnp.concatenate([seen, seen_other], axis=1),
        1,
        1,
    ).astype(bf16)
    grad_proj = dot(
        jnp.concatenate(
            [saved_own, saved_other, *by_replica(last_own, last_other)], axis=1
        ),
        jnp.concatenate([early, early_other, both[0], both[1]], axis=1),
        1,
        1,
    ).astype(bf16)
    return (
        grad_proj.reshape(1, 2, own_in, width),
        grad_up[None],
        grad_down[None],
        input_grad.transpose(2, 0, 1)[None],
    )


def solution(mesh):
    in_specs = (
        P("section", "replica", None, "tensor"),
        P("section", "replica", None),
        P("section", "replica", None),
        P("section", "replica", "tensor"),
        P(None, "replica", "tensor"),
        P("section", None, ("tensor", "replica"), None),
        P("section", None, ("tensor", "replica")),
        P("section", ("tensor", "replica"), None),
    )
    out_specs = (
        P("section", None, ("tensor", "replica"), None),
        P("section", None, ("tensor", "replica")),
        P("section", ("tensor", "replica"), None),
        P("section", "replica", None, "tensor"),
    )
    return jax.shard_map(body, mesh=mesh, in_specs=in_specs, out_specs=out_specs, check_vma=False)
```

```python
import jax
import jax.numpy as jnp
from jax import lax
from jax.sharding import PartitionSpec as P

gelu_scale = 0.7978845608
gelu_cubic = 0.044715
f32 = jnp.float32
bf16 = jnp.bfloat16


def gelu_pair(pre_gelu):
    inner = gelu_scale * (pre_gelu + gelu_cubic * pre_gelu * pre_gelu * pre_gelu)
    tanh_part = jnp.tanh(inner)
    gelu_value = 0.5 * pre_gelu * (1.0 + tanh_part)
    gelu_slope = 0.5 * (1.0 + tanh_part) + 0.5 * pre_gelu * (
        1.0 - tanh_part * tanh_part
    ) * gelu_scale * (1.0 + 3.0 * gelu_cubic * pre_gelu * pre_gelu)
    return (gelu_value, gelu_slope)


def dot(a, b, ca=1, cb=0):
    return lax.dot_general(a, b, (((ca,), (cb,)), ((), ())), preferred_element_type=f32)


def swap(x):
    return lax.ppermute(x, "replica", [(0, 1), (1, 0)])


def tied(*values):
    return lax.optimization_barrier(values)


def gather(chunk, axes="tensor"):
    count = lax.axis_size(axes)
    spread = jnp.broadcast_to(chunk[None], (count, *chunk.shape))
    return lax.all_to_all(spread, axes, 0, 0)


def body(pool_inputs, pool_mixed, crop_ids, incoming, loss_grads, w_proj, w_up, w_down):
    section = lax.axis_index("section")
    sections = lax.axis_size("section")
    replica = lax.axis_index("replica")
    parts = lax.axis_size("tensor")
    half = sections // 2
    first = replica == 0
    is_top = section == sections - 1
    ticks, rows = crop_ids.shape[1:]
    pool = pool_mixed.shape[1]
    width = pool_mixed.shape[2]
    units = w_down.shape[1]
    own_in = w_proj.shape[2]
    chunk_rows = incoming.shape[2]

    def by_replica(own, other):
        return jnp.where(first, own, other), jnp.where(first, other, own)

    up_other = swap(w_up[0])
    down_other = swap(w_down[0])
    proj_other = swap(w_proj[0])

    chunk = incoming[0].T
    upstream = gather(chunk).reshape(width, rows)

    up = jnp.concatenate([w_up[0], up_other], axis=1)
    proj = jnp.concatenate(by_replica(w_proj[0], proj_other), axis=1).reshape(-1, width)

    places = jnp.arange(pool, dtype=jnp.int32)[:, None]
    pick = (crop_ids[0].reshape(1, -1) == places).astype(bf16)

    def picked(t):
        return pick[:, t * rows : (t + 1) * rows]

    pre = dot(up, pool_mixed[0], 0, 1)
    value, slope = gelu_pair(pre)
    active = value.astype(bf16)
    high = slope.astype(bf16)
    low = (slope - high.astype(f32)).astype(bf16)
    slopes = dot(high, pick) + dot(low, pick)
    down = jnp.concatenate([w_down[0], down_other], axis=0)

    def small_of(inputs, active_sent, ids_sent):
        saved = inputs.transpose(1, 2, 0)
        decoder = jnp.where(section < half, 0.0, 1.0).astype(bf16)
        saved = jnp.stack([saved[0], saved[1] * decoder])
        saved_first, saved_second = saved[:, :own_in], saved[:, own_in:]
        saved_own = jnp.where(first, saved_first, saved_second).reshape(-1, pool)
        saved_sent = jnp.where(first, saved_second, saved_first).reshape(-1, pool)
        ids = jnp.broadcast_to(ids_sent.astype(bf16)[None], (16, rows))
        return saved_own, jnp.concatenate([saved_sent, active_sent, ids], axis=0)

    hiddens, grads, upstreams = [], [], []
    for t in range(ticks):
        upstreams.append(upstream)
        slope_now = slopes[:, t * rows : (t + 1) * rows]
        hidden = (dot(down, upstream) * slope_now).astype(bf16)
        hiddens.append(hidden)
        partial = dot(up, hidden).astype(bf16)
        if t + 1 == ticks:
            upstreams[-1], _ = tied(upstream, partial)
            seen = dot(jnp.concatenate(upstreams, axis=1), pick, 1, 1).astype(bf16)
            seen_other = swap(seen)
        terms = lax.all_to_all(partial.reshape(parts, chunk_rows, rows), "tensor", 0, 0)
        mixed_chunk = (
            jnp.sum(terms.astype(f32), axis=0) + chunk.astype(f32)
        ).astype(bf16)
        if t + 1 < ticks:
            mixed_grad = gather(mixed_chunk).reshape(width, rows)
            grads.append(mixed_grad)
            skip_grad = dot(proj[chunk_rows:], mixed_grad).astype(bf16)
            mirrored = lax.ppermute(
                skip_grad,
                "section",
                [(i, sections - 1 - i) for i in range(half, sections)],
            )
            later_grad, _ = tied(mixed_grad, skip_grad)
            above = lax.ppermute(
                dot(proj[:chunk_rows], later_grad).astype(bf16),
                "section",
                [(i, i - 1) for i in range(1, sections)],
            )
            if t == 0:
                down_own, down_late, _ = tied(w_down[0], down_other, skip_grad)
                (down,) = tied(jnp.concatenate([down_own, down_late], axis=0))
                mixed_sent, _ = tied(pool_mixed[0], skip_grad)
                sent = swap(mixed_sent)
                inputs, active_late, ids_late, _ = tied(
                    pool_inputs[0], active, crop_ids, skip_grad
                )
                saved_own, small = small_of(
                    inputs, active_late[units:], ids_late[0, ticks - 1]
                )
                small_other = swap(small)
            elif t + 2 == ticks:
                ids_late, _ = tied(crop_ids, skip_grad)
                picks = (ids_late[0, : t + 1].reshape(1, -1) == places).astype(bf16)
                early = dot(jnp.concatenate(grads, axis=1), picks, 1, 1)
                early = early.astype(bf16)
                sent = swap(early)
            summed = (above.astype(f32) + mirrored.astype(f32)).astype(bf16)
            chunk = jnp.where(is_top, loss_grads[t].T, summed)
            upstream = gather(chunk).reshape(width, rows)
            if t == 0:
                upstream, mixed_other, small_other = tied(upstream, sent, small_other)
            elif t + 2 == ticks:
                upstream, early_other = tied(upstream, sent)
                upstream, saved_own, small_other = tied(upstream, saved_own, small_other)
                count = saved_own.shape[0]
                saved_other = small_other[:count]
                active_other = small_other[count : count + units]
                ids_other = small_other[count + units].astype(jnp.int32)
                pick_other = (ids_other[None, :] == places).astype(bf16)
                last_own = dot(saved_own, picked(ticks - 1)).astype(bf16)
                last_other = dot(saved_other, pick_other).astype(bf16)
        else:
            spread = dot(jnp.concatenate(hiddens, axis=1), pick, 1, 1).astype(bf16)
            spread_other = swap(spread[units:])
            both = gather(mixed_chunk, ("replica", "tensor")).reshape(2, width, rows)
            input_grad = jnp.where(first, dot(proj, both[0]), dot(proj, both[1]))
            input_grad = input_grad.astype(bf16).reshape(2, chunk_rows, rows)

    grad_up = dot(
        jnp.concatenate([pool_mixed[0], mixed_other], axis=0),
        jnp.concatenate([spread[:units], spread_other], axis=1),
        0,
        1,
    ).astype(bf16)
    grad_down = dot(
        jnp.concatenate([active[:units], active_other], axis=1),
        jnp.concatenate([seen, seen_other], axis=1),
        1,
        1,
    ).astype(bf16)
    grad_proj = dot(
        jnp.concatenate(
            [saved_own, saved_other, *by_replica(last_own, last_other)], axis=1
        ),
        jnp.concatenate([early, early_other, both[0], both[1]], axis=1),
        1,
        1,
    ).astype(bf16)
    return (
        grad_proj.reshape(1, 2, own_in, width),
        grad_up[None],
        grad_down[None],
        input_grad.transpose(2, 0, 1)[None],
    )


def solution(mesh):
    in_specs = (
        P("section", "replica", None, "tensor"),
        P("section", "replica", None),
        P("section", "replica", None),
        P("section", "replica", "tensor"),
        P(None, "replica", "tensor"),
        P("section", None, ("tensor", "replica"), None),
        P("section", None, ("tensor", "replica")),
        P("section", ("tensor", "replica"), None),
    )
    out_specs = (
        P("section", None, ("tensor", "replica"), None),
        P("section", None, ("tensor", "replica")),
        P("section", ("tensor", "replica"), None),
        P("section", "replica", None, "tensor"),
    )
    return jax.shard_map(body, mesh=mesh, in_specs=in_specs, out_specs=out_specs, check_vma=False)
```

```python
import jax
import jax.numpy as jnp
from jax import lax
from jax.sharding import PartitionSpec as P

gelu_scale = 0.7978845608
gelu_cubic = 0.044715
f32 = jnp.float32
bf16 = jnp.bfloat16


def gelu_pair(pre_gelu):
    inner = gelu_scale * (pre_gelu + gelu_cubic * pre_gelu * pre_gelu * pre_gelu)
    tanh_part = jnp.tanh(inner)
    gelu_value = 0.5 * pre_gelu * (1.0 + tanh_part)
    gelu_slope = 0.5 * (1.0 + tanh_part) + 0.5 * pre_gelu * (
        1.0 - tanh_part * tanh_part
    ) * gelu_scale * (1.0 + 3.0 * gelu_cubic * pre_gelu * pre_gelu)
    return (gelu_value, gelu_slope)


def dot(a, b, ca=1, cb=0):
    return lax.dot_general(a, b, (((ca,), (cb,)), ((), ())), preferred_element_type=f32)


def swap(x):
    return lax.ppermute(x, "replica", [(0, 1), (1, 0)])


def tied(*values):
    return lax.optimization_barrier(values)


def gather(chunk, axes="tensor"):
    count = lax.axis_size(axes)
    spread = jnp.broadcast_to(chunk[None], (count, *chunk.shape))
    return lax.all_to_all(spread, axes, 0, 0)


def body(pool_inputs, pool_mixed, crop_ids, incoming, loss_grads, w_proj, w_up, w_down):
    section = lax.axis_index("section")
    sections = lax.axis_size("section")
    replica = lax.axis_index("replica")
    parts = lax.axis_size("tensor")
    half = sections // 2
    first = replica == 0
    is_top = section == sections - 1
    ticks, rows = crop_ids.shape[1:]
    pool = pool_mixed.shape[1]
    width = pool_mixed.shape[2]
    units = w_down.shape[1]
    own_in = w_proj.shape[2]
    chunk_rows = incoming.shape[2]

    def by_replica(own, other):
        return jnp.where(first, own, other), jnp.where(first, other, own)

    up_other = swap(w_up[0])
    down_other = swap(w_down[0])
    proj_other = swap(w_proj[0])

    chunk = incoming[0].T
    upstream = gather(chunk).reshape(width, rows)

    up = jnp.concatenate([w_up[0], up_other], axis=1)
    proj = jnp.concatenate(by_replica(w_proj[0], proj_other), axis=1).reshape(-1, width)

    places = jnp.arange(pool, dtype=jnp.int32)[:, None]
    pick = (crop_ids[0].reshape(1, -1) == places).astype(bf16)

    def picked(t):
        return pick[:, t * rows : (t + 1) * rows]

    pre = dot(up, pool_mixed[0], 0, 1)
    value, slope = gelu_pair(pre)
    active = value.astype(bf16)
    high = slope.astype(bf16)
    low = (slope - high.astype(f32)).astype(bf16)
    slopes = dot(high, pick) + dot(low, pick)
    down = jnp.concatenate([w_down[0], down_other], axis=0)

    def small_of(inputs, active_sent, ids_sent):
        saved = inputs.transpose(1, 2, 0)
        decoder = jnp.where(section < half, 0.0, 1.0).astype(bf16)
        saved = jnp.stack([saved[0], saved[1] * decoder])
        saved_first, saved_second = saved[:, :own_in], saved[:, own_in:]
        saved_own = jnp.where(first, saved_first, saved_second).reshape(-1, pool)
        saved_sent = jnp.where(first, saved_second, saved_first).reshape(-1, pool)
        ids = jnp.broadcast_to(ids_sent.astype(bf16)[None], (16, rows))
        return saved_own, jnp.concatenate([saved_sent, active_sent, ids], axis=0)

    hiddens, grads, upstreams = [], [], []

    def scattered(parts_of, start):
        ids_late, _ = tied(crop_ids, skip_grad)
        ids_late = ids_late[0, start : start + len(parts_of)].reshape(1, -1)
        picks = (ids_late == places).astype(bf16)
        return dot(jnp.concatenate(parts_of, axis=1), picks, 1, 1)

    for t in range(ticks):
        upstreams.append(upstream)
        slope_now = slopes[:, t * rows : (t + 1) * rows]
        hidden = (dot(down, upstream) * slope_now).astype(bf16)
        hiddens.append(hidden)
        partial = dot(up, hidden).astype(bf16)
        if t + 1 == ticks:
            upstreams[-1], _ = tied(upstream, partial)
            seen = dot(jnp.concatenate(upstreams, axis=1), pick, 1, 1).astype(bf16)
            seen_other = swap(seen)
        terms = lax.all_to_all(partial.reshape(parts, chunk_rows, rows), "tensor", 0, 0)
        mixed_chunk = (
            jnp.sum(terms.astype(f32), axis=0) + chunk.astype(f32)
        ).astype(bf16)
        if t + 1 < ticks:
            mixed_grad = gather(mixed_chunk).reshape(width, rows)
            grads.append(mixed_grad)
            skip_grad = dot(proj[chunk_rows:], mixed_grad).astype(bf16)
            mirrored = lax.ppermute(
                skip_grad,
                "section",
                [(i, sections - 1 - i) for i in range(half, sections)],
            )
            later_grad, _ = tied(mixed_grad, skip_grad)
            above = lax.ppermute(
                dot(proj[:chunk_rows], later_grad).astype(bf16),
                "section",
                [(i, i - 1) for i in range(1, sections)],
            )
            if t == 0:
                down_own, down_late, _ = tied(w_down[0], down_other, skip_grad)
                (down,) = tied(jnp.concatenate([down_own, down_late], axis=0))
                mixed_sent, _ = tied(pool_mixed[0], skip_grad)
                sent = swap(mixed_sent)
                inputs, active_late, ids_late, _ = tied(
                    pool_inputs[0], active, crop_ids, skip_grad
                )
                saved_own, small = small_of(
                    inputs, active_late[units:], ids_late[0, ticks - 1]
                )
                small_other = swap(small)
            elif t + 3 == ticks:
                first_part = scattered(grads, 0)
            elif t + 2 == ticks:
                early = first_part + scattered(grads[t:], t)
                early = early.astype(bf16)
                sent = swap(early)
            summed = (above.astype(f32) + mirrored.astype(f32)).astype(bf16)
            chunk = jnp.where(is_top, loss_grads[t].T, summed)
            if t + 3 == ticks:
                chunk, first_part = tied(chunk, first_part)
            upstream = gather(chunk).reshape(width, rows)
            if t == 0:
                upstream, mixed_other, small_other = tied(upstream, sent, small_other)
            elif t + 2 == ticks:
                upstream, early_other = tied(upstream, sent)
                upstream, saved_own, small_other = tied(upstream, saved_own, small_other)
                count = saved_own.shape[0]
                saved_other = small_other[:count]
                active_other = small_other[count : count + units]
                ids_other = small_other[count + units].astype(jnp.int32)
                pick_other = (ids_other[None, :] == places).astype(bf16)
                last_own = dot(saved_own, picked(ticks - 1)).astype(bf16)
                last_other = dot(saved_other, pick_other).astype(bf16)
        else:
            spread = dot(jnp.concatenate(hiddens, axis=1), pick, 1, 1).astype(bf16)
            spread_other = swap(spread[units:])
            both = gather(mixed_chunk, ("replica", "tensor")).reshape(2, width, rows)
            input_grad = jnp.where(first, dot(proj, both[0]), dot(proj, both[1]))
            input_grad = input_grad.astype(bf16).reshape(2, chunk_rows, rows)

    grad_up = dot(
        jnp.concatenate([pool_mixed[0], mixed_other], axis=0),
        jnp.concatenate([spread[:units], spread_other], axis=1),
        0,
        1,
    ).astype(bf16)
    grad_down = dot(
        jnp.concatenate([active[:units], active_other], axis=1),
        jnp.concatenate([seen, seen_other], axis=1),
        1,
        1,
    ).astype(bf16)
    grad_proj = dot(
        jnp.concatenate(
            [saved_own, saved_other, *by_replica(last_own, last_other)], axis=1
        ),
        jnp.concatenate([early, early_other, both[0], both[1]], axis=1),
        1,
        1,
    ).astype(bf16)
    return (
        grad_proj.reshape(1, 2, own_in, width),
        grad_up[None],
        grad_down[None],
        input_grad.transpose(2, 0, 1)[None],
    )


def solution(mesh):
    in_specs = (
        P("section", "replica", None, "tensor"),
        P("section", "replica", None),
        P("section", "replica", None),
        P("section", "replica", "tensor"),
        P(None, "replica", "tensor"),
        P("section", None, ("tensor", "replica"), None),
        P("section", None, ("tensor", "replica")),
        P("section", ("tensor", "replica"), None),
    )
    out_specs = (
        P("section", None, ("tensor", "replica"), None),
        P("section", None, ("tensor", "replica")),
        P("section", ("tensor", "replica"), None),
        P("section", "replica", None, "tensor"),
    )
    return jax.shard_map(body, mesh=mesh, in_specs=in_specs, out_specs=out_specs, check_vma=False)
```
